32 devices in a mesh: section: 2 (over y), ctx: 4 (over z), dp: 4 (over x, core).
Axes of the slice: x: 2, y: 2, z: 4, core: 2. Of those that a mesh axis runs over, the one named last changes fastest.
Arguments:
- cotangent: bfloat16 [4, 512, 4096], P('dp', 'ctx'), may hold values from -6 to 6
- activations: bfloat16 [2, 4, 512, 4096], P('section', 'dp', 'ctx'), may hold values from -6 to 6
- gate_values: bfloat16 [2, 4, 512, 4096], P('section', 'dp', 'ctx'), may hold values from -6 to 6
- residue: float32 [2, 4096], P('section'), may hold values from -1 to 1
- skip_gain: float32 [2, 4096], P('section'), may hold values from -3 to 3
- decay_rate: float32 [2, 4096], P('section'), may hold values from 9.765625e-05 to 0.03
Outputs:
- input_grads: bfloat16 [2, 4, 512, 4096], P('section', 'dp', 'ctx')
- grad_residue: float32 [2, 4096], P('section')
- grad_skip: float32 [2, 4096], P('section')
The draws below stay inside these ranges and needn't reach their ends.
All inputs are finite; a program needn't handle non-finite values.
Results may differ from the reference program's by a relative error of at most 0.0079.
Values may be sent and summed in bfloat16 or wider, within the bound.
A program may use at most 64 MiB of HBM per device.

```python
import math
import jax
import jax.numpy as jnp
from jax import lax

D = 4096
TOK_DEV = 128
SEQ_LEN = 512
SEQS = 4
LAYERS = 2
N_CTX = 4


def steps_of(rng, shape, split, least, high):
    level = 1.0
    for axis_at, blocks in split:
        heights = jax.random.uniform(jax.random.fold_in(jax.random.fold_in(rng, 6), axis_at), (blocks,), jnp.float32, least / len(split), high / len(split))
        level = level * jnp.repeat(jnp.exp(heights), shape[axis_at] // blocks).reshape((-1,) + (1,) * (len(shape) - 1 - axis_at))
    return level


def bell_draw(own_key, dims, width, reach, cuts=(), held_as=jnp.bfloat16):
    gain = steps_of(own_key, dims, cuts, -0.22, 0.18) if cuts else 1.0
    values = jax.random.normal(own_key, dims, jnp.float32) * width * gain
    return jnp.minimum(jnp.maximum(values, -reach), reach).astype(held_as)


def setup_inputs(seed: int = 0) -> dict:
    arg_keys = jax.random.split(jax.random.key(seed), 7)
    cotangent = bell_draw(arg_keys[0], (SEQS, SEQ_LEN, D), 1.0, 6.0, ((0, 4), (1, 4)))
    activations = bell_draw(arg_keys[1], (LAYERS, SEQS, SEQ_LEN, D), 1.0, 6.0, ((0, 2), (1, 4), (2, 4)))
    gate_values = bell_draw(arg_keys[2], (LAYERS, SEQS, SEQ_LEN, D), 1.0, 6.0, ((0, 2), (1, 4), (2, 4)))
    residue = bell_draw(arg_keys[3], (LAYERS, D), (1.5 / (TOK_DEV * N_CTX) ** 0.5), 1.0, ((0, 2),), jnp.float32)
    skip_gain = bell_draw(arg_keys[4], (LAYERS, D), 0.5, 3.0, ((0, 2),), jnp.float32)
    decay_rate = jnp.clip(jnp.exp(math.log(0.03) - 5.727499 * jax.random.uniform(arg_keys[5], (LAYERS, D), jnp.float32) ** steps_of(arg_keys[5], (LAYERS, D), ((0, 2),), -0.2, 0.2)), 9.765625145519152e-05, 0.03)
    return {"cotangent": cotangent, "activations": activations, "gate_values": gate_values, "residue": residue, "skip_gain": skip_gain, "decay_rate": decay_rate}


def compose_maps(earlier, later_map):
    return (earlier[0] * later_map[0], later_map[1] + later_map[0] * earlier[1])

def reverse_scan(values, decay, axis):
    flipped = jnp.flip(values, axis)
    factors = jnp.broadcast_to(decay, values.shape)
    _, output = lax.associative_scan(compose_maps, (factors, flipped), axis=axis)
    return jnp.flip(output, axis)

def reference(cotangent, activations, gate_values, residue, skip_gain, decay_rate):
    factor = 1.0 / math.sqrt(SEQS * SEQ_LEN)
    current = cotangent
    input_list = [None] * LAYERS
    residue_list = [None] * LAYERS
    skip_list = [None] * LAYERS
    for layer_index in range(LAYERS - 1, -1, -1):
        weighted = (current.astype(jnp.float32) * gate_values[layer_index].astype(jnp.float32)).astype(jnp.bfloat16)
        widened = lax.optimization_barrier(weighted).astype(jnp.float32)
        decay = jnp.exp(-decay_rate[layer_index])
        carried = lax.map(lambda seq_values: reverse_scan(seq_values, decay, 0), widened)
        carried = lax.optimization_barrier(carried.astype(jnp.bfloat16)).astype(jnp.float32)
        branch = residue[layer_index] * carried + skip_gain[layer_index] * widened
        current = (current.astype(jnp.float32) + branch).astype(jnp.bfloat16)
        saved = activations[layer_index].astype(jnp.float32)
        input_list[layer_index] = current
        residue_list[layer_index] = lax.optimization_barrier(jnp.sum(saved * carried, axis=(0, 1))) * factor
        skip_list[layer_index] = lax.optimization_barrier(jnp.sum(saved * widened, axis=(0, 1))) * factor
    return (jnp.stack(input_list), jnp.stack(residue_list), jnp.stack(skip_list))
```

```python
import functools
import math

import jax
import jax.numpy as jnp
from jax import lax
from jax.experimental import pallas as pl
from jax.experimental.pallas import tpu as pltpu
from jax.sharding import PartitionSpec as P

MESH = pl.DeviceIdType.MESH
F32 = jnp.float32
BF16 = jnp.bfloat16
WIDTH = 512


def kernel(sizes, cot, act, gate, residue, skip, rate, out, g_res, g_skip,
           cot_v, act_v, gate_v, inc_v, recv_v, out_v, y_v, pos_v, neg_v, pos_up, neg_up, tri,
           res_up, skip_up, rate_up, pre_out, pre_in, msg, tot,
           load_sem, store_sem, par_s, par_r, y_s, y_r, pre_s, pre_r, msg_s, msg_r, tot_s, tot_r):
    sections, n_ctx, n_dp, width, factor = sizes
    tokens, channels = cot.shape
    chunks = channels // width
    sec, ctx, dp = (lax.axis_index(a) for a in ("section", "ctx", "dp"))
    is_top = sec == sections - 1
    is_second = sec == sections - 2

    loads = [
        pltpu.make_async_copy(src, dst, load_sem.at[n])
        for n, (src, dst) in enumerate(((gate, gate_v), (cot, cot_v), (act, act_v)))
    ]
    for load in loads:
        load.start()

    barrier = pltpu.get_barrier_semaphore()
    for j in range(1, n_ctx):
        pl.semaphore_signal(barrier, inc=1, device_id={"ctx": lax.rem(ctx + j, n_ctx)}, device_id_type=MESH)
    for j in range(1, n_dp):
        pl.semaphore_signal(barrier, inc=1, device_id={"dp": lax.rem(dp + j, n_dp)}, device_id_type=MESH)

    @pl.when(sec > 0)
    def _():
        pl.semaphore_signal(barrier, inc=1, device_id={"section": sec - 1}, device_id_type=MESH)

    @pl.when(sec < sections - 1)
    def _():
        pl.semaphore_signal(barrier, inc=1, device_id={"section": sec + 1}, device_id_type=MESH)

    ends = jnp.where(sec > 0, 1, 0) + jnp.where(sec < sections - 1, 1, 0)
    pl.semaphore_wait(barrier, n_ctx - 1 + n_dp - 1 + ends)

    def cols(i):
        return pl.ds(pl.multiple_of(i * width, width), width)

    def below(src, dst, send, recv):
        return pltpu.make_async_remote_copy(
            src_ref=src, dst_ref=dst, send_sem=send, recv_sem=recv,
            device_id={"section": lax.rem(sec + sections - 1, sections)}, device_id_type=MESH)

    def params_down():
        return [
            below(src, dst, par_s.at[n], par_r.at[n])
            for n, (src, dst) in enumerate(((residue, res_up), (skip, skip_up), (rate, rate_up)))
        ]

    def gate_down(i):
        return below(gate.at[:, cols(i)], recv_v.at[:, cols(i)], y_s.at[i], y_r.at[i])

    def out_down(i):
        return below(out_v.at[:, cols(i)], recv_v.at[:, cols(i)], y_s.at[i], y_r.at[i])

    def prefix_down(i):
        return below(pre_out.at[:, cols(i)], pre_in.at[:, cols(i)], pre_s.at[i], pre_r.at[i])

    def message(j, i, slot):
        peer = lax.rem(ctx + j, n_ctx)
        return pltpu.make_async_remote_copy(
            src_ref=msg.at[slot, :, cols(i)], dst_ref=msg.at[slot, :, cols(i)],
            send_sem=msg_s.at[j, i], recv_sem=msg_r.at[slot, i],
            device_id={"ctx": peer}, device_id_type=MESH)

    def total(j, i, slot):
        peer = lax.rem(dp + j, n_dp)
        return pltpu.make_async_remote_copy(
            src_ref=tot.at[slot, :, cols(i)], dst_ref=tot.at[slot, :, cols(i)],
            send_sem=tot_s.at[j, i], recv_sem=tot_r.at[slot, i],
            device_id={"dp": peer}, device_id_type=MESH)

    def stored(i):
        return pltpu.make_async_copy(out_v.at[:, cols(i)], out.at[:, cols(i)], store_sem.at[i])

    half = (chunks + 1) // 2

    @pl.when(is_top)
    def _():
        for copy in params_down():
            copy.start()
        pl.loop(0, half)(lambda i: gate_down(i).start())

    at = lax.broadcasted_iota(jnp.int32, (tokens, tokens), 0)
    of = lax.broadcasted_iota(jnp.int32, (tokens, tokens), 1)
    upper = jnp.where(of >= at, 1.0, 0.0).astype(BF16)
    tri[:, :tokens] = upper
    tri[:, tokens:] = upper

    def tables(rate_ref, pos_ref, neg_ref):
        @pl.loop(0, chunks)
        def _(i):
            steps = lax.broadcasted_iota(jnp.int32, (tokens, width), 0).astype(F32)
            powers = steps * rate_ref[:, cols(i)]
            pos_ref[:, cols(i)] = jnp.exp(powers)
            neg_ref[:, cols(i)] = jnp.exp(-powers)

    def suffix_sums(scaled):
        high = scaled.astype(BF16)
        low = (scaled - high.astype(F32)).astype(BF16)
        both = jnp.concatenate([high, low], axis=0)
        return jnp.dot(tri[...], both, preferred_element_type=F32)

    def weigh(incoming, gates):
        return (incoming * gates).astype(BF16).astype(F32)

    def result(incoming, weighted, sums, row, pos, res, gain):
        carried = (pos * (sums + row)).astype(BF16).astype(F32)
        return (incoming + (res * carried + gain * weighted)).astype(BF16)

    def arrive(i):
        gate_down(i).wait_recv()
        c = cols(i)

        @pl.when(is_second)
        def _():
            prefix_down(i).wait_recv()
            incoming = cot_v[:, c].astype(F32)
            weighted = weigh(incoming, recv_v[:, c].astype(F32))
            sums = suffix_sums(neg_up[:, c] * weighted)
            inc_v[:, c] = result(incoming, weighted, sums, pre_in[:, c], pos_up[:, c], res_up[:, c], skip_up[:, c])

        if sections > 2:
            @pl.when(jnp.logical_not(is_second))
            def _():
                inc_v[:, c] = recv_v[:, c]

    def front(i, inc_ref):
        c = cols(i)
        weighted = weigh(inc_ref[:, c].astype(F32), gate_v[:, c].astype(F32))
        sums = suffix_sums(neg_v[:, c] * weighted)
        y_v[:, c] = sums
        saved = act_v[:, c].astype(F32)
        lifted = saved * pos_v[:, c]
        fade = jnp.exp(rate[:, c] * -float(tokens))
        msg[ctx, 0:1, c] = sums[0:1]
        msg[ctx, 1:2, c] = jnp.sum(lifted * sums, axis=0, keepdims=True)
        msg[ctx, 2:3, c] = jnp.sum(lifted, axis=0, keepdims=True) * fade
        msg[ctx, 3:4, c] = jnp.sum(saved * weighted, axis=0, keepdims=True)
        for j in range(1, n_ctx):
            message(j, i, ctx).start()

    def back(i, inc_ref, top):
        c = cols(i)
        for j in range(1, n_ctx):
            message(j, i, lax.rem(ctx + j, n_ctx)).wait_recv()
        fade = jnp.exp(rate[:, c] * -float(tokens))
        after = jnp.zeros((1, width), F32)
        entering, total_res, total_skip = after, after, after
        for k in reversed(range(n_ctx)):
            total_res += msg[k, 1:2, c] + msg[k, 2:3, c] * after
            total_skip += msg[k, 3:4, c]
            entering = jnp.where(ctx == k, after, entering)
            after = msg[k, 0:1, c] + fade * after
        tot[dp, 0:1, c] = total_res
        tot[dp, 1:2, c] = total_skip
        for j in range(1, n_dp):
            total(j, i, dp).start()
        row = fade * entering
        if top:
            pre_out[:, c] = row
            prefix_down(i).start()
        incoming = inc_ref[:, c].astype(F32)
        weighted = weigh(incoming, gate_v[:, c].astype(F32))
        out_v[:, c] = result(incoming, weighted, y_v[:, c], row, pos_v[:, c], residue[:, c], skip[:, c])
        stored(i).start()
        if sections > 2 and not top:
            @pl.when(sec > 0)
            def _():
                out_down(i).start()

    tables(rate, pos_v, neg_v)
    for load in loads:
        load.wait()

    @pl.when(is_top)
    def _():
        pl.loop(0, chunks)(lambda i: front(i, cot_v))
        pl.loop(0, chunks)(lambda i: back(i, cot_v, True))
        pl.loop(half, chunks)(lambda i: gate_down(i).start())

    @pl.when(jnp.logical_not(is_top))
    def _():
        @pl.when(is_second)
        def _():
            for copy in params_down():
                copy.wait_recv()
            tables(rate_up, pos_up, neg_up)

        arrive(0)
        front(0, inc_v)

        @pl.loop(1, chunks)
        def _(i):
            arrive(i)
            front(i, inc_v)
            back(i - 1, inc_v, False)

        back(chunks - 1, inc_v, False)

    @pl.loop(0, chunks)
    def _(i):
        for j in range(1, n_dp):
            total(j, i, lax.rem(dp + j, n_dp)).wait_recv()
        c = cols(i)
        sums = tot[0, :, c]
        for k in range(1, n_dp):
            sums += tot[k, :, c]
        sums *= factor
        g_res[:, c] = sums[0:1]
        g_skip[:, c] = sums[1:2]

    @pl.loop(0, chunks)
    def _(i):
        for j in range(1, n_ctx):
            message(j, i, ctx).wait_send()
        for j in range(1, n_dp):
            total(j, i, dp).wait_send()
        stored(i).wait()

    @pl.when(is_top)
    def _():
        for copy in params_down():
            copy.wait_send()

        @pl.loop(0, chunks)
        def _(i):
            prefix_down(i).wait_send()
            gate_down(i).wait_send()

    if sections > 2:
        @pl.when(jnp.logical_and(sec > 0, jnp.logical_not(is_top)))
        def _():
            pl.loop(0, chunks)(lambda i: out_down(i).wait_send())


def on_device(cotangent, activations, gate_values, residue, skip_gain, decay_rate):
    sections, n_ctx, n_dp = (lax.axis_size(a) for a in ("section", "ctx", "dp"))
    tokens, channels = cotangent.shape[-2:]
    factor = 1.0 / math.sqrt(n_dp * n_ctx * tokens)
    width = math.gcd(WIDTH, channels)
    chunks = channels // width
    sizes = (sections, n_ctx, n_dp, width, factor)
    block = (tokens, channels)
    anywhere = pl.BlockSpec(memory_space=pl.ANY)
    inside = pl.BlockSpec(memory_space=pltpu.VMEM)
    row = jax.ShapeDtypeStruct((1, channels), F32)
    dma = pltpu.SemaphoreType.DMA
    result, g_res, g_skip = pl.pallas_call(
        functools.partial(kernel, sizes),
        out_shape=(jax.ShapeDtypeStruct(block, BF16), row, row),
        in_specs=[anywhere] * 3 + [inside] * 3,
        out_specs=(anywhere, inside, inside),
        scratch_shapes=[pltpu.VMEM(block, BF16)] * 6
        + [pltpu.VMEM(block, F32)] * 5
        + [pltpu.VMEM((tokens, 2 * tokens), BF16)]
        + [pltpu.VMEM((1, channels), F32)] * 5
        + [pltpu.VMEM((n_ctx, 4, channels), F32), pltpu.VMEM((n_dp, 2, channels), F32)]
        + [dma((3,)), dma((chunks,)), dma((3,)), dma((3,))]
        + [dma((chunks,))] * 4
        + [dma((n_ctx, chunks))] * 2
        + [dma((n_dp, chunks))] * 2,
        compiler_params=pltpu.CompilerParams(
            collective_id=0, has_side_effects=True, vmem_limit_bytes=40 * 1024 * 1024),
    )(cotangent.reshape(block), activations.reshape(block), gate_values.reshape(block),
      residue, skip_gain, decay_rate)
    return result.reshape(activations.shape), g_res, g_skip


def solution(mesh):
    return jax.shard_map(
        on_device,
        mesh=mesh,
        in_specs=(
            P("dp", "ctx", None),
            P("section", "dp", "ctx", None),
            P("section", "dp", "ctx", None),
            P("section", None),
            P("section", None),
            P("section", None),
        ),
        out_specs=(P("section", "dp", "ctx", None), P("section", None), P("section", None)),
        check_vma=False,
    )
```

```python
import functools
import math

import jax
import jax.numpy as jnp
from jax import lax
from jax.experimental import pallas as pl
from jax.experimental.pallas import tpu as pltpu
from jax.sharding import PartitionSpec as P

MESH = pl.DeviceIdType.MESH
F32 = jnp.float32
BF16 = jnp.bfloat16
WIDTH = 512
LEAD = 3
LAG = 1


def kernel(sizes, cot, act, gate, residue_h, skip_h, rate_h, out, g_res, g_skip,
           cot_v, act_v, gate_v, inc_v, recv_v, out_v, y_v, pos_v, neg_v, pos_up, neg_up, tri,
           residue, skip, rate, res_up, skip_up, rate_up, pre_out, pre_in, heads, msg, tot,
           load_sem, store_sem, par_s, par_r, y_s, y_r, pre_s, pre_r, head_s, head_r, msg_s, msg_r, tot_s, tot_r):
    sections, n_ctx, n_dp, width, factor = sizes
    tokens, channels = cot.shape
    chunks = channels // width
    sec, ctx, dp = (lax.axis_index(a) for a in ("section", "ctx", "dp"))
    is_top = sec == sections - 1
    is_second = sec == sections - 2

    loads = [
        pltpu.make_async_copy(src, dst, load_sem.at[n])
        for n, (src, dst) in enumerate((
            (gate, gate_v), (cot, cot_v), (rate_h, rate), (residue_h, residue), (skip_h, skip), (act, act_v)))
    ]
    for load in loads:
        load.start()

    barrier = pltpu.get_barrier_semaphore()
    for j in range(1, n_ctx):
        pl.semaphore_signal(barrier, inc=1, device_id={"ctx": lax.rem(ctx + j, n_ctx)}, device_id_type=MESH)
    for j in range(1, n_dp):
        pl.semaphore_signal(barrier, inc=1, device_id={"dp": lax.rem(dp + j, n_dp)}, device_id_type=MESH)

    @pl.when(sec > 0)
    def _():
        pl.semaphore_signal(barrier, inc=1, device_id={"section": sec - 1}, device_id_type=MESH)

    @pl.when(sec < sections - 1)
    def _():
        pl.semaphore_signal(barrier, inc=1, device_id={"section": sec + 1}, device_id_type=MESH)

    ends = jnp.where(sec > 0, 1, 0) + jnp.where(sec < sections - 1, 1, 0)
    pl.semaphore_wait(barrier, n_ctx - 1 + n_dp - 1 + ends)

    def cols(i):
        return pl.ds(pl.multiple_of(i * width, width), width)

    def below(src, dst, send, recv):
        return pltpu.make_async_remote_copy(
            src_ref=src, dst_ref=dst, send_sem=send, recv_sem=recv,
            device_id={"section": lax.rem(sec + sections - 1, sections)}, device_id_type=MESH)

    def params_down():
        return [
            below(src, dst, par_s.at[n], par_r.at[n])
            for n, (src, dst) in enumerate(((residue_h, res_up), (skip_h, skip_up), (rate_h, rate_up)))
        ]

    def gate_down(i):
        return below(gate.at[:, cols(i)], recv_v.at[:, cols(i)], y_s.at[i], y_r.at[i])

    def out_down(i):
        return below(out_v.at[:, cols(i)], recv_v.at[:, cols(i)], y_s.at[i], y_r.at[i])

    def prefix_down():
        return below(pre_out, pre_in, pre_s, pre_r)

    def head(j, slot):
        return pltpu.make_async_remote_copy(
            src_ref=heads.at[slot], dst_ref=heads.at[slot],
            send_sem=head_s.at[j], recv_sem=head_r.at[slot],
            device_id={"ctx": lax.rem(ctx + j, n_ctx)}, device_id_type=MESH)

    def message(j, i, slot):
        peer = lax.rem(ctx + j, n_ctx)
        return pltpu.make_async_remote_copy(
            src_ref=msg.at[slot, :, cols(i)], dst_ref=msg.at[slot, :, cols(i)],
            send_sem=msg_s.at[j, i], recv_sem=msg_r.at[slot, i],
            device_id={"ctx": peer}, device_id_type=MESH)

    def total(j, i, slot):
        peer = lax.rem(dp + j, n_dp)
        return pltpu.make_async_remote_copy(
            src_ref=tot.at[slot, :, cols(i)], dst_ref=tot.at[slot, :, cols(i)],
            send_sem=tot_s.at[j, i], recv_sem=tot_r.at[slot, i],
            device_id={"dp": peer}, device_id_type=MESH)

    def stored(i):
        return pltpu.make_async_copy(out_v.at[:, cols(i)], out.at[:, cols(i)], store_sem.at[i])

    lead = min(LEAD, chunks)
    lag = min(LAG, chunks)

    @pl.when(is_top)
    def _():
        for copy in params_down():
            copy.start()
        pl.loop(0, lead)(lambda i: gate_down(i).start())

    at = lax.broadcasted_iota(jnp.int32, (tokens, tokens), 0)
    of = lax.broadcasted_iota(jnp.int32, (tokens, tokens), 1)
    upper = jnp.where(of >= at, 1.0, 0.0).astype(BF16)
    tri[:, :tokens] = upper
    tri[:, tokens:] = upper

    def tables(rate_ref, pos_ref, neg_ref):
        @pl.loop(0, chunks)
        def _(i):
            steps = lax.broadcasted_iota(jnp.int32, (tokens, width), 0).astype(F32)
            powers = steps * rate_ref[:, cols(i)]
            pos_ref[:, cols(i)] = jnp.exp(powers)
            neg_ref[:, cols(i)] = jnp.exp(-powers)

    def suffix_sums(scaled):
        high = scaled.astype(BF16)
        low = (scaled - high.astype(F32)).astype(BF16)
        both = jnp.concatenate([high, low], axis=0)
        return jnp.dot(tri[...], both, preferred_element_type=F32)

    def weigh(incoming, gates):
        return (incoming * gates).astype(BF16).astype(F32)

    def result(incoming, weighted, sums, row, pos, res, gain):
        carried = (pos * (sums + row)).astype(BF16).astype(F32)
        return (incoming + (res * carried + gain * weighted)).astype(BF16)

    def arrive(i):
        gate_down(i).wait_recv()
        c = cols(i)

        @pl.when(is_second)
        def _():
            incoming = cot_v[:, c].astype(F32)
            weighted = weigh(incoming, recv_v[:, c].astype(F32))
            sums = suffix_sums(neg_up[:, c] * weighted)
            inc_v[:, c] = result(incoming, weighted, sums, pre_in[:, c], pos_up[:, c], res_up[:, c], skip_up[:, c])

        if sections > 2:
            @pl.when(jnp.logical_not(is_second))
            def _():
                inc_v[:, c] = recv_v[:, c]

    def fade_of(c):
        return jnp.exp(rate[:, c] * -float(tokens))

    def column_sum(values):
        return jnp.sum(values, axis=0, keepdims=True)

    def announce(i, *rows):
        for n, row in enumerate(rows):
            msg[ctx, n:n + 1, cols(i)] = row
        for j in range(1, n_ctx):
            message(j, i, ctx).start()

    def whole_block(i):
        c = cols(i)
        incoming = cot_v[:, c].astype(F32)
        weighted = weigh(incoming, gate_v[:, c].astype(F32))
        sums = suffix_sums(neg_v[:, c] * weighted)
        carried = (pos_v[:, c] * (sums + pre_out[:, c])).astype(BF16).astype(F32)
        out_v[:, c] = (incoming + (residue[:, c] * carried + skip[:, c] * weighted)).astype(BF16)
        stored(i).start()
        saved = act_v[:, c].astype(F32)
        none = jnp.zeros((1, width), F32)
        announce(i, none, column_sum(saved * carried), none, column_sum(saved * weighted))

    def front(i):
        c = cols(i)
        weighted = weigh(inc_v[:, c].astype(F32), gate_v[:, c].astype(F32))
        sums = suffix_sums(neg_v[:, c] * weighted)
        y_v[:, c] = sums
        saved = act_v[:, c].astype(F32)
        lifted = saved * pos_v[:, c]
        announce(i, sums[0:1], column_sum(lifted * sums), column_sum(lifted) * fade_of(c), column_sum(saved * weighted))

    def combine(i):
        c = cols(i)
        for j in range(1, n_ctx):
            message(j, i, lax.rem(ctx + j, n_ctx)).wait_recv()
        fade = fade_of(c)
        after = jnp.zeros((1, width), F32)
        entering, total_res, total_skip = after, after, after
        for k in reversed(range(n_ctx)):
            total_res += msg[k, 1:2, c] + msg[k, 2:3, c] * after
            total_skip += msg[k, 3:4, c]
            entering = jnp.where(ctx == k, after, entering)
            after = msg[k, 0:1, c] + fade * after
        tot[dp, 0:1, c] = total_res
        tot[dp, 1:2, c] = total_skip
        for j in range(1, n_dp):
            total(j, i, dp).start()
        return fade * entering

    def back(i):
        c = cols(i)
        row = combine(i)
        incoming = inc_v[:, c].astype(F32)
        weighted = weigh(incoming, gate_v[:, c].astype(F32))
        out_v[:, c] = result(incoming, weighted, y_v[:, c], row, pos_v[:, c], residue[:, c], skip[:, c])
        stored(i).start()
        if sections > 2:
            @pl.when(sec > 0)
            def _():
                out_down(i).start()

    for load in loads[:-1]:
        load.wait()

    @pl.when(is_top)
    def _():
        steps = lax.broadcasted_iota(jnp.int32, (tokens, width), 0).astype(F32)

        @pl.loop(0, chunks)
        def _(i):
            c = cols(i)
            factors = jnp.exp(-(steps * rate[:, c]))
            neg_v[:, c] = factors
            heads[ctx, 0:1, c] = column_sum(factors * weigh(cot_v[:, c].astype(F32), gate_v[:, c].astype(F32)))

        for j in range(1, n_ctx):
            head(j, ctx).start()

        @pl.loop(0, chunks)
        def _(i):
            pos_v[:, cols(i)] = jnp.exp(steps * rate[:, cols(i)])

        for j in range(1, n_ctx):
            head(j, lax.rem(ctx + j, n_ctx)).wait_recv()

        @pl.loop(0, chunks)
        def _(i):
            c = cols(i)
            fade = fade_of(c)
            after = jnp.zeros((1, width), F32)
            entering = after
            for k in reversed(range(n_ctx)):
                entering = jnp.where(ctx == k, after, entering)
                after = heads[k, :, c] + fade * after
            pre_out[:, c] = fade * entering

        prefix_down().start()
        pl.loop(lead, chunks)(lambda i: gate_down(i).start())
        loads[-1].wait()
        pl.loop(0, chunks)(whole_block)

        @pl.loop(0, chunks)
        def _(i):
            combine(i)

    @pl.when(jnp.logical_not(is_top))
    def _():
        tables(rate, pos_v, neg_v)
        loads[-1].wait()

        @pl.when(is_second)
        def _():
            for copy in params_down():
                copy.wait_recv()
            tables(rate_up, pos_up, neg_up)
            prefix_down().wait_recv()

        @pl.loop(0, lag)
        def _(i):
            arrive(i)
            front(i)

        @pl.loop(lag, chunks)
        def _(i):
            arrive(i)
            front(i)
            back(i - lag)

        pl.loop(chunks - lag, chunks)(back)

    @pl.loop(0, chunks)
    def _(i):
        for j in range(1, n_dp):
            total(j, i, lax.rem(dp + j, n_dp)).wait_recv()
        c = cols(i)
        sums = tot[0, :, c]
        for k in range(1, n_dp):
            sums += tot[k, :, c]
        sums *= factor
        g_res[:, c] = sums[0:1]
        g_skip[:, c] = sums[1:2]

    @pl.loop(0, chunks)
    def _(i):
        for j in range(1, n_ctx):
            message(j, i, ctx).wait_send()
        for j in range(1, n_dp):
            total(j, i, dp).wait_send()
        stored(i).wait()

    @pl.when(is_top)
    def _():
        for copy in params_down():
            copy.wait_send()
        prefix_down().wait_send()
        for j in range(1, n_ctx):
            head(j, ctx).wait_send()

        @pl.loop(0, chunks)
        def _(i):
            gate_down(i).wait_send()

    if sections > 2:
        @pl.when(jnp.logical_and(sec > 0, jnp.logical_not(is_top)))
        def _():
            pl.loop(0, chunks)(lambda i: out_down(i).wait_send())


def on_device(cotangent, activations, gate_values, residue, skip_gain, decay_rate):
    sections, n_ctx, n_dp = (lax.axis_size(a) for a in ("section", "ctx", "dp"))
    tokens, channels = cotangent.shape[-2:]
    factor = 1.0 / math.sqrt(n_dp * n_ctx * tokens)
    width = math.gcd(WIDTH, channels)
    chunks = channels // width
    sizes = (sections, n_ctx, n_dp, width, factor)
    block = (tokens, channels)
    anywhere = pl.BlockSpec(memory_space=pl.ANY)
    outside = pl.BlockSpec(memory_space=pltpu.HBM)
    inside = pl.BlockSpec(memory_space=pltpu.VMEM)
    row = jax.ShapeDtypeStruct((1, channels), F32)
    dma = pltpu.SemaphoreType.DMA
    result, g_res, g_skip = pl.pallas_call(
        functools.partial(kernel, sizes),
        out_shape=(jax.ShapeDtypeStruct(block, BF16), row, row),
        in_specs=[outside] * 6,
        out_specs=(anywhere, inside, inside),
        scratch_shapes=[pltpu.VMEM(block, BF16)] * 6
        + [pltpu.VMEM(block, F32)] * 5
        + [pltpu.VMEM((tokens, 2 * tokens), BF16)]
        + [pltpu.VMEM((1, channels), F32)] * 8
        + [pltpu.VMEM((n_ctx, 1, channels), F32)]
        + [pltpu.VMEM((n_ctx, 4, channels), F32), pltpu.VMEM((n_dp, 2, channels), F32)]
        + [dma((6,)), dma((chunks,)), dma((3,)), dma((3,)), dma((chunks,)), dma((chunks,)), dma, dma]
        + [dma((n_ctx,))] * 2
        + [dma((n_ctx, chunks))] * 2
        + [dma((n_dp, chunks))] * 2,
        compiler_params=pltpu.CompilerParams(
            collective_id=0, has_side_effects=True, vmem_limit_bytes=60 * 1024 * 1024),
    )(cotangent.reshape(block), activations.reshape(block), gate_values.reshape(block),
      residue, skip_gain, decay_rate)
    return result.reshape(activations.shape), g_res, g_skip


def solution(mesh):
    return jax.shard_map(
        on_device,
        mesh=mesh,
        in_specs=(
            P("dp", "ctx", None),
            P("section", "dp", "ctx", None),
            P("section", "dp", "ctx", None),
            P("section", None),
            P("section", None),
            P("section", None),
        ),
        out_specs=(P("section", "dp", "ctx", None), P("section", None), P("section", None)),
        check_vma=False,
    )
```

```python
import functools
import math

import jax
import jax.numpy as jnp
from jax import lax
from jax.experimental import pallas as pl
from jax.experimental.pallas import tpu as pltpu
from jax.sharding import PartitionSpec as P

MESH = pl.DeviceIdType.MESH
F32 = jnp.float32
BF16 = jnp.bfloat16
WIDTH = 512
LEAD = 2
LAG = 2


def kernel(sizes, cot, act, gate, residue_h, skip_h, rate_h, out, g_res, g_skip,
           cot_v, act_v, gate_v, inc_v, recv_v, out_v, y_v, pos_v, neg_v, pos_up, neg_up, tri,
           residue, skip, rate, res_up, skip_up, rate_up, pre_out, pre_in, heads, msg, tot,
           load_sem, store_sem, par_s, par_r, y_s, y_r, pre_s, pre_r, head_s, head_r, msg_s, msg_r, tot_s, tot_r):
    sections, n_ctx, n_dp, width, factor = sizes
    tokens, channels = cot.shape
    chunks = channels // width
    sec, ctx, dp = (lax.axis_index(a) for a in ("section", "ctx", "dp"))
    is_top = sec == sections - 1
    is_second = sec == sections - 2

    loads = [
        pltpu.make_async_copy(src, dst, load_sem.at[n])
        for n, (src, dst) in enumerate((
            (gate, gate_v), (cot, cot_v), (rate_h, rate), (residue_h, residue), (skip_h, skip), (act, act_v)))
    ]
    for load in loads:
        load.start()

    barrier = pltpu.get_barrier_semaphore()
    for j in range(1, n_ctx):
        pl.semaphore_signal(barrier, inc=1, device_id={"ctx": lax.rem(ctx + j, n_ctx)}, device_id_type=MESH)
    for j in range(1, n_dp):
        pl.semaphore_signal(barrier, inc=1, device_id={"dp": lax.rem(dp + j, n_dp)}, device_id_type=MESH)

    @pl.when(sec > 0)
    def _():
        pl.semaphore_signal(barrier, inc=1, device_id={"section": sec - 1}, device_id_type=MESH)

    @pl.when(sec < sections - 1)
    def _():
        pl.semaphore_signal(barrier, inc=1, device_id={"section": sec + 1}, device_id_type=MESH)

    ends = jnp.where(sec > 0, 1, 0) + jnp.where(sec < sections - 1, 1, 0)
    pl.semaphore_wait(barrier, n_ctx - 1 + n_dp - 1 + ends)

    def cols(i):
        return pl.ds(pl.multiple_of(i * width, width), width)

    def below(src, dst, send, recv):
        return pltpu.make_async_remote_copy(
            src_ref=src, dst_ref=dst, send_sem=send, recv_sem=recv,
            device_id={"section": lax.rem(sec + sections - 1, sections)}, device_id_type=MESH)

    def params_down():
        return [
            below(src, dst, par_s.at[n], par_r.at[n])
            for n, (src, dst) in enumerate(((residue_h, res_up), (skip_h, skip_up), (rate_h, rate_up)))
        ]

    def gate_down(i):
        return below(gate.at[:, cols(i)], recv_v.at[:, cols(i)], y_s.at[i], y_r.at[i])

    def out_down(i):
        return below(out_v.at[:, cols(i)], recv_v.at[:, cols(i)], y_s.at[i], y_r.at[i])

    def prefix_down():
        return below(pre_out, pre_in, pre_s, pre_r)

    def head(j, slot):
        return pltpu.make_async_remote_copy(
            src_ref=heads.at[slot], dst_ref=heads.at[slot],
            send_sem=head_s.at[j], recv_sem=head_r.at[slot],
            device_id={"ctx": lax.rem(ctx + j, n_ctx)}, device_id_type=MESH)

    def message(j, i, slot):
        peer = lax.rem(ctx + j, n_ctx)
        return pltpu.make_async_remote_copy(
            src_ref=msg.at[slot, :, cols(i)], dst_ref=msg.at[slot, :, cols(i)],
            send_sem=msg_s.at[j, i], recv_sem=msg_r.at[slot, i],
            device_id={"ctx": peer}, device_id_type=MESH)

    def total(j, slot):
        peer = lax.rem(dp + j, n_dp)
        return pltpu.make_async_remote_copy(
            src_ref=tot.at[slot], dst_ref=tot.at[slot],
            send_sem=tot_s.at[j], recv_sem=tot_r.at[slot],
            device_id={"dp": peer}, device_id_type=MESH)

    def stored(i):
        return pltpu.make_async_copy(out_v.at[:, cols(i)], out.at[:, cols(i)], store_sem.at[i])

    lead = min(LEAD, chunks)
    lag = min(LAG, chunks)

    @pl.when(is_top)
    def _():
        for copy in params_down():
            copy.start()
        pl.loop(0, lead)(lambda i: gate_down(i).start())

    at = lax.broadcasted_iota(jnp.int32, (tokens, tokens), 0)
    of = lax.broadcasted_iota(jnp.int32, (tokens, tokens), 1)
    upper = jnp.where(of >= at, 1.0, 0.0).astype(BF16)
    tri[:, :tokens] = upper
    tri[:, tokens:] = upper

    def tables(rate_ref, pos_ref, neg_ref):
        @pl.loop(0, chunks)
        def _(i):
            steps = lax.broadcasted_iota(jnp.int32, (tokens, width), 0).astype(F32)
            powers = steps * rate_ref[:, cols(i)]
            pos_ref[:, cols(i)] = jnp.exp(powers)
            neg_ref[:, cols(i)] = jnp.exp(-powers)

    def suffix_sums(scaled):
        high = scaled.astype(BF16)
        low = (scaled - high.astype(F32)).astype(BF16)
        both = jnp.concatenate([high, low], axis=0)
        return jnp.dot(tri[...], both, preferred_element_type=F32)

    def weigh(incoming, gates):
        return (incoming * gates).astype(BF16).astype(F32)

    def result(incoming, weighted, sums, row, pos, res, gain):
        carried = (pos * (sums + row)).astype(BF16).astype(F32)
        return (incoming + (res * carried + gain * weighted)).astype(BF16)

    def arrive(i):
        gate_down(i).wait_recv()
        c = cols(i)

        @pl.when(is_second)
        def _():
            incoming = cot_v[:, c].astype(F32)
            weighted = weigh(incoming, recv_v[:, c].astype(F32))
            sums = suffix_sums(neg_up[:, c] * weighted)
            inc_v[:, c] = result(incoming, weighted, sums, pre_in[:, c], pos_up[:, c], res_up[:, c], skip_up[:, c])

        if sections > 2:
            @pl.when(jnp.logical_not(is_second))
            def _():
                inc_v[:, c] = recv_v[:, c]

    def fade_of(c):
        return jnp.exp(rate[:, c] * -float(tokens))

    def column_sum(values):
        return jnp.sum(values, axis=0, keepdims=True)

    def announce(i, *rows):
        for n, row in enumerate(rows):
            msg[ctx, n:n + 1, cols(i)] = row
        for j in range(1, n_ctx):
            message(j, i, ctx).start()

    def whole_block(i):
        c = cols(i)
        incoming = cot_v[:, c].astype(F32)
        weighted = weigh(incoming, gate_v[:, c].astype(F32))
        sums = suffix_sums(neg_v[:, c] * weighted)
        carried = (pos_v[:, c] * (sums + pre_out[:, c])).astype(BF16).astype(F32)
        out_v[:, c] = (incoming + (residue[:, c] * carried + skip[:, c] * weighted)).astype(BF16)
        stored(i).start()
        saved = act_v[:, c].astype(F32)
        none = jnp.zeros((1, width), F32)
        announce(i, none, column_sum(saved * carried), none, column_sum(saved * weighted))

    def front(i):
        c = cols(i)
        weighted = weigh(inc_v[:, c].astype(F32), gate_v[:, c].astype(F32))
        sums = suffix_sums(neg_v[:, c] * weighted)
        y_v[:, c] = sums
        saved = act_v[:, c].astype(F32)
        lifted = saved * pos_v[:, c]
        announce(i, sums[0:1], column_sum(lifted * sums), column_sum(lifted) * fade_of(c), column_sum(saved * weighted))

    def combine(i):
        c = cols(i)
        for j in range(1, n_ctx):
            message(j, i, lax.rem(ctx + j, n_ctx)).wait_recv()
        fade = fade_of(c)
        after = jnp.zeros((1, width), F32)
        entering, total_res, total_skip = after, after, after
        for k in reversed(range(n_ctx)):
            total_res += msg[k, 1:2, c] + msg[k, 2:3, c] * after
            total_skip += msg[k, 3:4, c]
            entering = jnp.where(ctx == k, after, entering)
            after = msg[k, 0:1, c] + fade * after
        tot[dp, 0:1, c] = total_res
        tot[dp, 1:2, c] = total_skip
        return fade * entering

    def back(i):
        c = cols(i)
        row = combine(i)
        incoming = inc_v[:, c].astype(F32)
        weighted = weigh(incoming, gate_v[:, c].astype(F32))
        out_v[:, c] = result(incoming, weighted, y_v[:, c], row, pos_v[:, c], residue[:, c], skip[:, c])
        stored(i).start()
        if sections > 2:
            @pl.when(sec > 0)
            def _():
                out_down(i).start()

    for load in loads[:-1]:
        load.wait()

    @pl.when(is_top)
    def _():
        steps = lax.broadcasted_iota(jnp.int32, (tokens, width), 0).astype(F32)

        @pl.loop(0, chunks)
        def _(i):
            c = cols(i)
            factors = jnp.exp(-(steps * rate[:, c]))
            neg_v[:, c] = factors
            heads[ctx, 0:1, c] = column_sum(factors * weigh(cot_v[:, c].astype(F32), gate_v[:, c].astype(F32)))

        for j in range(1, n_ctx):
            head(j, ctx).start()

        @pl.loop(0, chunks)
        def _(i):
            pos_v[:, cols(i)] = jnp.exp(steps * rate[:, cols(i)])

        for j in range(1, n_ctx):
            head(j, lax.rem(ctx + j, n_ctx)).wait_recv()

        @pl.loop(0, chunks)
        def _(i):
            c = cols(i)
            fade = fade_of(c)
            after = jnp.zeros((1, width), F32)
            entering = after
            for k in reversed(range(n_ctx)):
                entering = jnp.where(ctx == k, after, entering)
                after = heads[k, :, c] + fade * after
            pre_out[:, c] = fade * entering

        prefix_down().start()
        pl.loop(lead, chunks)(lambda i: gate_down(i).start())
        loads[-1].wait()
        pl.loop(0, chunks)(whole_block)

        @pl.loop(0, chunks)
        def _(i):
            combine(i)

    @pl.when(jnp.logical_not(is_top))
    def _():
        tables(rate, pos_v, neg_v)
        loads[-1].wait()

        @pl.when(is_second)
        def _():
            for copy in params_down():
                copy.wait_recv()
            tables(rate_up, pos_up, neg_up)
            prefix_down().wait_recv()

        @pl.loop(0, lag)
        def _(i):
            arrive(i)
            front(i)

        @pl.loop(lag, chunks)
        def _(i):
            arrive(i)
            front(i)
            back(i - lag)

        pl.loop(chunks - lag, chunks)(back)

    for j in range(1, n_dp):
        total(j, dp).start()
    for j in range(1, n_dp):
        total(j, lax.rem(dp + j, n_dp)).wait_recv()

    @pl.loop(0, chunks)
    def _(i):
        c = cols(i)
        sums = tot[0, :, c]
        for k in range(1, n_dp):
            sums += tot[k, :, c]
        sums *= factor
        g_res[:, c] = sums[0:1]
        g_skip[:, c] = sums[1:2]

    @pl.loop(0, chunks)
    def _(i):
        for j in range(1, n_ctx):
            message(j, i, ctx).wait_send()
        stored(i).wait()

    for j in range(1, n_dp):
        total(j, dp).wait_send()

    @pl.when(is_top)
    def _():
        for copy in params_down():
            copy.wait_send()
        prefix_down().wait_send()
        for j in range(1, n_ctx):
            head(j, ctx).wait_send()

        @pl.loop(0, chunks)
        def _(i):
            gate_down(i).wait_send()

    if sections > 2:
        @pl.when(jnp.logical_and(sec > 0, jnp.logical_not(is_top)))
        def _():
            pl.loop(0, chunks)(lambda i: out_down(i).wait_send())


def on_device(cotangent, activations, gate_values, residue, skip_gain, decay_rate):
    sections, n_ctx, n_dp = (lax.axis_size(a) for a in ("section", "ctx", "dp"))
    tokens, channels = cotangent.shape[-2:]
    factor = 1.0 / math.sqrt(n_dp * n_ctx * tokens)
    width = math.gcd(WIDTH, channels)
    chunks = channels // width
    sizes = (sections, n_ctx, n_dp, width, factor)
    block = (tokens, channels)
    anywhere = pl.BlockSpec(memory_space=pl.ANY)
    outside = pl.BlockSpec(memory_space=pltpu.HBM)
    inside = pl.BlockSpec(memory_space=pltpu.VMEM)
    row = jax.ShapeDtypeStruct((1, channels), F32)
    dma = pltpu.SemaphoreType.DMA
    result, g_res, g_skip = pl.pallas_call(
        functools.partial(kernel, sizes),
        out_shape=(jax.ShapeDtypeStruct(block, BF16), row, row),
        in_specs=[outside] * 6,
        out_specs=(anywhere, inside, inside),
        scratch_shapes=[pltpu.VMEM(block, BF16)] * 6
        + [pltpu.VMEM(block, F32)] * 5
        + [pltpu.VMEM((tokens, 2 * tokens), BF16)]
        + [pltpu.VMEM((1, channels), F32)] * 8
        + [pltpu.VMEM((n_ctx, 1, channels), F32)]
        + [pltpu.VMEM((n_ctx, 4, channels), F32), pltpu.VMEM((n_dp, 2, channels), F32)]
        + [dma((6,)), dma((chunks,)), dma((3,)), dma((3,)), dma((chunks,)), dma((chunks,)), dma, dma]
        + [dma((n_ctx,))] * 2
        + [dma((n_ctx, chunks))] * 2
        + [dma((n_dp,))] * 2,
        compiler_params=pltpu.CompilerParams(
            collective_id=0, has_side_effects=True, vmem_limit_bytes=60 * 1024 * 1024),
    )(cotangent.reshape(block), activations.reshape(block), gate_values.reshape(block),
      residue, skip_gain, decay_rate)
    return result.reshape(activations.shape), g_res, g_skip


def solution(mesh):
    return jax.shard_map(
        on_device,
        mesh=mesh,
        in_specs=(
            P("dp", "ctx", None),
            P("section", "dp", "ctx", None),
            P("section", "dp", "ctx", None),
            P("section", None),
            P("section", None),
            P("section", None),
        ),
        out_specs=(P("section", "dp", "ctx", None), P("section", None), P("section", None)),
        check_vma=False,
    )
```
